128 devices in a mesh: ctx: 8 (over x_hi, z), exp: 16 (over x_lo, y, core).
Axes of the slice: x: 4 (x_hi: 2, x_lo: 2; x = x_hi * 2 + x_lo), y: 4, z: 4, core: 2. Of those that a mesh axis runs over, the one named last changes fastest.
Arguments:
- queries: bfloat16 [16, 1024, 6144], P('exp', 'ctx'), may hold values from -140 to 140
- keys_values: bfloat16 [16, 1024, 2048], P('exp', 'ctx'), may hold values from -4.5 to 4.5
- doc_ids: int32 [16, 1024], P('exp', 'ctx'), may hold values from 0 to 15, never falling along the last dimension, each value on 1 to 512 neighbouring positions
- expert_ids: int32 [16, 1024, 1], P('exp', 'ctx'), may hold values from 0 to 15; in each aligned block of 128 rows (0 to 127, 128 to 255, ..., all dimensions but the last counted through in order) at most 10 rows name the same one
- gate_probs: float32 [16, 1024, 1], P('exp', 'ctx'), may hold values from 0.25 to 1
- w_gate: bfloat16 [16, 6144, 5376], P('exp', None, 'ctx'), may hold values from -0.078125 to 0.078125
- w_down: bfloat16 [16, 5376, 6144], P('exp', 'ctx'), may hold values from -0.078125 to 0.078125
Outputs:
- layer_out: bfloat16 [16, 1024, 6144], P('exp', 'ctx')
The draws below stay inside these ranges and needn't reach their ends.
Inputs may be any that keep to these rules, and one draw needn't show every extreme that they name: `doc_ids`: document numbers never fall along a sequence; a document covers at most 512 positions and one covers exactly that many. `expert_ids`: within the 128 tokens of one device (aligned blocks of the flattened sequences), no expert is named more than 10 times, a bound that some block reaches.
All inputs are finite; a program needn't handle non-finite values.
Results may differ from the reference program's by a relative error of at most 0.01.
Values may be sent and summed in bfloat16 or wider, within the bound.
No kernel may reach another device: no remote copies, remote signals or barrier semaphores. Data moves between devices by JAX's collectives and lax.ppermute only.
A program may use at most 192 MiB of HBM per device.

```python
import math
import jax
import jax.numpy as jnp
import numpy as np
from jax import lax

D = 6144
QUERY_HEADS = 48
KEY_VALUE_HEADS = 8
HEAD_WIDTH = 128
FF = 5376
TOPK = 1
TOK_DEV = 128
QUERY_PER_KEY = 6
EXPERTS = 16
PACKED_COUNT = 16
PACKED_LENGTH = 1024
CAP = 10
N_CTX = 8
N_EXP = 16


def shared_draw(key):
    unscaled_sample = jnp.clip(jax.random.normal(key, (PACKED_COUNT, PACKED_LENGTH, 2 * KEY_VALUE_HEADS * HEAD_WIDTH), jnp.float32), -4.5, 4.5)
    return unscaled_sample


def draw_keys_values(key, part):
    unscaled_sample = shared_draw(key)
    return unscaled_sample.astype(jnp.bfloat16)


def draw_queries(key, part):
    key = jax.random.fold_in(key, 4)
    base_draw = jnp.clip(jax.random.normal(key, (PACKED_COUNT, PACKED_LENGTH, QUERY_HEADS * HEAD_WIDTH), jnp.float32), -6.0, 6.0)
    return base_draw.astype(jnp.bfloat16)


def block_scale(stream_key, extent, cuts, smallest, largest):
    gain = 1.0
    for axis_at, parts in cuts:
        heights = jax.random.uniform(jax.random.fold_in(jax.random.fold_in(stream_key, 6), axis_at), (parts,), jnp.float32, smallest / len(cuts), largest / len(cuts))
        gain = gain * jnp.repeat(jnp.exp(heights), extent[axis_at] // parts).reshape((-1,) + (1,) * (len(extent) - 1 - axis_at))
    return gain


def split_up(number_of, total, bound, slope):
    loads = [(1 << 20) // math.isqrt(grade ** slope) + 1 for grade in range(2, number_of + 1)]
    surplus, given = total - bound - (number_of - 1), [1] * (number_of - 1)
    while surplus > 0:
        free = [i for i in range(number_of - 1) if given[i] < bound]
        mass, left = sum([loads[i] for i in free]), surplus
        for i in free:
            addition = min(bound - given[i], max(1, left * loads[i] // mass), surplus)
            given[i] = given[i] + addition
            surplus = surplus - addition
    return np.array([bound] + given)


def ragged(own_key, number_of, total, limit, lean):
    if number_of == 2:
        one = jax.random.randint(own_key, (), max(1, total - limit), min(limit, total - 1) + 1)
        return jnp.stack([one, total - one])
    sizes = jnp.asarray(split_up(number_of, total, limit, lean), jnp.int32)
    twos = (number_of - 1) // 2
    donor, taker = sizes[1:1 + 2 * twos:2], sizes[2:2 + 2 * twos:2]
    slack = jnp.minimum(donor - 1, limit - taker)
    moved = jax.random.randint(jax.random.fold_in(own_key, 1), (twos,), 0, 1 << 20) % (slack + 1)
    sizes = sizes.at[1:1 + 2 * twos:2].set(donor - moved).at[2:2 + 2 * twos:2].set(taker + moved)
    return sizes[jax.random.permutation(jax.random.fold_in(own_key, 2), number_of)]


def assign_block(own_key, own, number, rows, count, top, most, slope):
    ranking = jax.random.permutation(own_key, count)
    crowded, ordinary = load_shares(count, rows * top, most, slope, True), load_shares(count, rows * top, most, slope, False)
    places = jnp.arange(count)

    def named(lengths, turn):
        used = int((lengths > 0).sum())
        fixed = max(1, used // 4)
        passed = fixed + (places - fixed + turn * (used - fixed)) % max(1, count - fixed)
        return jnp.zeros((count,), jnp.int32).at[ranking[jnp.where(places < fixed, places, passed)]].set(jnp.asarray(lengths, jnp.int32))

    lengths = jnp.where(number % 4 == 0, named(crowded, number // 4), named(ordinary, number - number // 4 - 1))
    mixed = jax.random.permutation(jax.random.fold_in(own, 3), count)
    donor, taker = mixed[0:count // 2 * 2:2], mixed[1:count // 2 * 2:2]
    slack = jnp.minimum(lengths[donor] - 1, most - lengths[taker]) // 2
    slack = jnp.where((donor == ranking[0]) | (taker == ranking[0]) | (lengths[taker] == 0), 0, jnp.maximum(slack, 0))
    passed = jax.random.randint(jax.random.fold_in(own, 4), (count // 2,), 0, 1 << 20) % (slack + 1)
    lengths = lengths.at[donor].add(-passed).at[taker].add(passed)
    labels = jnp.searchsorted(jnp.cumsum(lengths), jnp.arange(rows * top), side="right").astype(jnp.int32)
    listing = labels.reshape(top, rows).T
    listing = listing[jax.random.permutation(jax.random.fold_in(own, 1), rows)]
    turn = jax.random.randint(jax.random.fold_in(own, 2), (rows, 1), 0, top)
    return jnp.take_along_axis(listing, (jnp.arange(top)[None, :] + turn) % top, axis=1)


def load_shares(number_of, total, reach, skew, full):
    weights = [(1 << 20) // math.isqrt(standing ** skew) + 1 for standing in range(1, number_of + 1)]
    largest = reach if full else min(reach, max(-(-total // number_of), total * weights[0] // sum(weights)))
    least = 1 if total - largest >= number_of - 1 else 0
    holding, surplus = [largest] + [least] * (number_of - 1), total - largest - least * (number_of - 1)
    while surplus > 0:
        candidates = [i for i in range(1, number_of) if holding[i] < largest] or [i for i in range(1, number_of) if holding[i] < reach]
        whole, remaining = sum([weights[i] for i in candidates]), surplus
        for i in candidates:
            addition = min(reach - holding[i], max(1, remaining * weights[i] // whole), surplus)
            holding[i] = holding[i] + addition
            surplus = surplus - addition
    return np.array(holding)


def gaussian(stream_key, extent, deviation, most, pieces=(), held_as=jnp.bfloat16):
    entries = deviation * jax.random.normal(stream_key, extent, jnp.float32)
    if pieces:
        entries = entries * block_scale(stream_key, extent, pieces, -0.22, 0.18)
    return jnp.clip(entries, -most, most).astype(held_as)


def setup_inputs(seed: int = 0) -> dict:
    streams_of = jax.random.split(jax.random.key(seed), 8)
    queries = draw_queries(jax.random.fold_in(streams_of[7], 71), 0)
    keys_values = draw_keys_values(jax.random.fold_in(streams_of[7], 71), 0)
    doc_ids = jax.vmap(lambda own: jnp.searchsorted(jnp.cumsum(ragged(own, 2 * N_CTX, PACKED_LENGTH, PACKED_LENGTH // 2, 2)), jnp.arange(PACKED_LENGTH), side="right"))(jax.random.split(streams_of[2], PACKED_COUNT)).reshape((PACKED_COUNT, PACKED_LENGTH)).astype(jnp.int32)
    expert_ids_keys = jax.random.split(jax.random.fold_in(streams_of[3], 1), PACKED_COUNT * PACKED_LENGTH // TOK_DEV)
    expert_ids_turns = jax.random.permutation(jax.random.fold_in(streams_of[3], 3), PACKED_COUNT * PACKED_LENGTH // TOK_DEV)
    expert_ids = jax.vmap(lambda own, number: assign_block(jax.random.fold_in(streams_of[3], 2), own, number, TOK_DEV, EXPERTS, TOPK, CAP, 2))(expert_ids_keys, expert_ids_turns).reshape((PACKED_COUNT, PACKED_LENGTH, TOPK))
    gate_probs = jnp.clip(0.25 + 0.75 * jax.random.uniform(streams_of[4], (PACKED_COUNT, PACKED_LENGTH, TOPK), jnp.float32) ** block_scale(streams_of[4], (PACKED_COUNT, PACKED_LENGTH, TOPK), ((0, 16), (1, 8)), -0.2, 0.2), 0.25, 1.0)
    w_gate = gaussian(streams_of[5], (EXPERTS, D, FF), D ** -0.5, 0.078125, ((0, 16), (2, 8)))
    w_down = gaussian(streams_of[6], (EXPERTS, FF, D), FF ** -0.5, 0.078125, ((0, 16), (1, 8)))
    return dict(queries=queries, keys_values=keys_values, doc_ids=doc_ids, expert_ids=expert_ids, gate_probs=gate_probs, w_gate=w_gate, w_down=w_down)


def attend_one(packed):
    sequence_queries, sequence_keys, seq_docs = packed
    sequence_length = sequence_queries.shape[0]
    query_head_rows = sequence_queries.astype(jnp.float32).reshape(sequence_length, KEY_VALUE_HEADS, QUERY_PER_KEY, HEAD_WIDTH)
    key_head_rows = sequence_keys[:, :KEY_VALUE_HEADS * HEAD_WIDTH].astype(jnp.float32).reshape(sequence_length, KEY_VALUE_HEADS, HEAD_WIDTH)
    value_head_rows = sequence_keys[:, KEY_VALUE_HEADS * HEAD_WIDTH:].astype(jnp.float32).reshape(sequence_length, KEY_VALUE_HEADS, HEAD_WIDTH)
    scores = jnp.einsum('qhgd,khd->hgqk', query_head_rows, key_head_rows) * (1.0 / math.sqrt(HEAD_WIDTH))
    positions = jnp.arange(sequence_length, dtype=jnp.int32)
    allowed = (seq_docs[:, None] == seq_docs[None, :]) & (positions[None, :] <= positions[:, None])
    scores = jnp.where(allowed, scores, -1e+30)
    row_max = lax.optimization_barrier(jnp.max(scores, axis=-1, keepdims=True))
    weights = jnp.exp(scores - row_max)
    totals = lax.optimization_barrier(jnp.sum(weights, axis=-1))
    rounded = lax.optimization_barrier(weights.astype(jnp.bfloat16)).astype(jnp.float32)
    blended = jnp.einsum('hgqk,khd->qhgd', rounded, value_head_rows)
    blended = blended / jnp.transpose(totals, (2, 0, 1))[..., None]
    return blended.reshape(sequence_length, QUERY_HEADS * HEAD_WIDTH).astype(jnp.bfloat16)

def reference(queries, keys_values, doc_ids, expert_ids, gate_probs, w_gate, w_down):
    attended = lax.map(attend_one, (queries, keys_values, doc_ids))
    token_count = PACKED_COUNT * PACKED_LENGTH
    widened = attended.reshape(token_count, D).astype(jnp.float32)
    centered = widened - lax.optimization_barrier(jnp.mean(widened, axis=-1, keepdims=True))
    variance = lax.optimization_barrier(jnp.mean(centered * centered, axis=-1, keepdims=True))
    normed = (centered * lax.rsqrt(variance + 1e-05)).astype(jnp.bfloat16)
    routed = expert_ids.reshape(token_count, TOPK)
    router_weights = gate_probs.reshape(token_count, TOPK)
    most_rows = N_CTX * N_EXP * CAP
    unit_span = FF // N_CTX

    def one_expert(accumulated, expert):
        matches = routed == expert
        combine_weight = lax.optimization_barrier(jnp.sum(jnp.where(matches, router_weights, 0.0), axis=-1))
        picked = jnp.any(matches, axis=-1)
        positions = jnp.nonzero(picked, size=most_rows, fill_value=0)[0].astype(jnp.int32)
        live_mask = jnp.arange(most_rows, dtype=jnp.int32) < jnp.sum(picked.astype(jnp.int32))
        gathered = normed[positions]
        gate_matrix = w_gate[expert]
        down_matrix = w_down[expert]
        hidden = jax.nn.silu(jnp.dot(gathered, gate_matrix, preferred_element_type=jnp.float32)).astype(jnp.bfloat16)
        summed = jnp.zeros((most_rows, D), jnp.float32)
        for part_index in range(N_CTX):
            lower = part_index * unit_span
            partial_value = jnp.dot(hidden[:, lower:lower + unit_span], down_matrix[lower:lower + unit_span], preferred_element_type=jnp.float32)
            summed = summed + lax.optimization_barrier(partial_value.astype(jnp.bfloat16)).astype(jnp.float32)
        out_rows = lax.optimization_barrier(summed.astype(jnp.bfloat16)).astype(jnp.float32)
        scaled = out_rows * (combine_weight[positions] * live_mask.astype(jnp.float32))[:, None]
        return (accumulated.at[positions].add(scaled), None)
    accumulated, unused = lax.scan(one_expert, jnp.zeros((token_count, D), jnp.float32), jnp.arange(EXPERTS, dtype=jnp.int32))
    combined = widened + accumulated
    return combined.reshape(PACKED_COUNT, PACKED_LENGTH, D).astype(jnp.bfloat16)
```

```python
import math

import jax
import jax.numpy as jnp
from jax import lax
from jax.experimental import pallas as pl
from jax.experimental.pallas import tpu as pltpu
from jax.sharding import Mesh, PartitionSpec as P

D = 6144
HALF = D // 2
TOK = 128
KV_HEADS = 8
GROUP = 6
HW = 128
GW = GROUP * HW
WINDOW = 5
EXPERTS = 16
CAP = 10
MAIN = 8
FOLD = 4
UNIT = 672
PACK_ROWS = EXPERTS * MAIN
BLOCK_ROWS = EXPERTS * CAP
PIECES = (3072, 2048, 1024)
UNITS = (224, 112, 336)
VMEM = 50 * 1024 * 1024
PLANE = ("xl", "y", "xh")
HINT = pl.CostEstimate(flops=10**6, bytes_accessed=10**5, transcendentals=0)
BF = jnp.bfloat16
F32 = jnp.float32


def iota(shape, axis):
    return lax.broadcasted_iota(jnp.int32, shape, axis)


def dot(a, b):
    return jnp.dot(a, b, preferred_element_type=F32)


def dot_t(a, b):
    return lax.dot_general(a, b, (((1,), (1,)), ((), ())), preferred_element_type=F32)


def attend_kernel(place_ref, doc_ref, ecol_ref, erow_ref, q_ref, *refs):
    k_refs = refs[:WINDOW]
    v_refs = refs[WINDOW : 2 * WINDOW]
    d_refs = refs[2 * WINDOW : 3 * WINDOW]
    att_ref, send, bias, keys, values, held, scores, weights, totals = refs[3 * WINDOW :]
    head = pl.program_id(0)

    @pl.when(head == 0)
    def _():
        place = place_ref[0]
        mine = doc_ref[...]
        for n in range(WINDOW):
            same = mine == d_refs[n][...].astype(F32)
            if n == 0:
                ok = same & (iota((TOK, TOK), 1) <= iota((TOK, TOK), 0))
            else:
                ok = same & (iota((TOK, TOK), 0) * 0 + place >= n)
            bias[:, n * TOK : (n + 1) * TOK] = jnp.where(ok, 0.0, -1e30)

    for n in range(WINDOW):
        keys[n * TOK : (n + 1) * TOK, :] = k_refs[n][...]
        values[n * TOK : (n + 1) * TOK, :] = v_refs[n][...]
    stacked = jnp.concatenate([q_ref[:, i * HW : (i + 1) * HW] for i in range(GROUP)], axis=0)
    scores[...] = dot_t(stacked, keys[...])
    for i in range(GROUP):
        rows = slice(i * TOK, (i + 1) * TOK)
        s = scores[rows, :] * (math.log2(math.e) / math.sqrt(HW)) + bias[...]
        w = jnp.exp2(s - jnp.max(s, axis=1, keepdims=True))
        totals[rows, :] = jnp.sum(w, axis=1, keepdims=True)
        weights[rows, :] = w.astype(BF)
    blended = (dot(weights[...], values[...]) / totals[...]).astype(BF)
    for i in range(GROUP):
        o = blended[i * TOK : (i + 1) * TOK]
        att_ref[:, i * HW : (i + 1) * HW] = o
        held[head, :, i * HW : (i + 1) * HW] = o

    @pl.when(head == KV_HEADS - 1)
    def _():
        total = jnp.zeros((TOK, 1), F32)
        for g in range(KV_HEADS):
            total += jnp.sum(held[g].astype(F32), axis=1, keepdims=True)
        mean = total * (1.0 / D)
        square = jnp.zeros((TOK, 1), F32)
        for g in range(KV_HEADS):
            c = held[g].astype(F32) - mean
            square += jnp.sum(c * c, axis=1, keepdims=True)
        scale = lax.rsqrt(square * (1.0 / D) + 1e-05)
        for g in range(KV_HEADS):
            held[g] = ((held[g].astype(F32) - mean) * scale).astype(BF)
        experts = erow_ref[...]
        earlier = (ecol_ref[...] == experts) & (iota((TOK, TOK), 0) < iota((TOK, TOK), 1))
        slot = experts * CAP + jnp.sum(earlier.astype(jnp.int32), axis=0, keepdims=True)
        row = iota((2 * PACK_ROWS, TOK), 0)
        expert, half, r = row // (2 * MAIN), row // MAIN % 2, row % MAIN
        hit = slot == expert * CAP + r
        main_hot = jnp.concatenate(
            [(hit & (half == h)).astype(F32).astype(BF) for h in range(2)], axis=1
        )
        hit = slot == expert * CAP + MAIN + r % 2
        extra_hot = jnp.concatenate(
            [
                (hit & (half == n // FOLD) & (r // 2 == n % FOLD)).astype(F32).astype(BF)
                for n in range(KV_HEADS)
            ],
            axis=1,
        )
        for o in range(FOLD):
            pair = jnp.concatenate([held[o], held[FOLD + o]], axis=0)
            send[:, o * GW : (o + 1) * GW] = dot(main_hot, pair).astype(BF)
        every = jnp.concatenate([held[n] for n in range(KV_HEADS)], axis=0)
        send[:, HALF:] = dot(extra_hot, every).astype(BF)


def attend(place, doc_col, expert_col, expert_row, queries, blocks):
    def whole(shape):
        return pl.BlockSpec(shape, lambda g: (0, 0))

    in_specs = [
        pl.BlockSpec(memory_space=pltpu.SMEM),
        whole((TOK, 1)),
        whole((TOK, 1)),
        whole((1, TOK)),
        pl.BlockSpec((TOK, GW), lambda g: (0, g)),
    ]
    in_specs += [pl.BlockSpec((TOK, HW), lambda g: (0, g))] * WINDOW
    in_specs += [pl.BlockSpec((TOK, HW), lambda g: (0, KV_HEADS + g))] * WINDOW
    in_specs += [pl.BlockSpec((TOK, HW), lambda g: (0, 2 * KV_HEADS))] * WINDOW
    return pl.pallas_call(
        attend_kernel,
        grid=(KV_HEADS,),
        in_specs=in_specs,
        out_specs=[
            pl.BlockSpec((TOK, GW), lambda g: (0, g)),
            whole((2 * PACK_ROWS, HALF + GW)),
        ],
        out_shape=[
            jax.ShapeDtypeStruct((TOK, D), BF),
            jax.ShapeDtypeStruct((2 * PACK_ROWS, HALF + GW), BF),
        ],
        scratch_shapes=[
            pltpu.VMEM((TOK, WINDOW * TOK), F32),
            pltpu.VMEM((WINDOW * TOK, HW), BF),
            pltpu.VMEM((WINDOW * TOK, HW), BF),
            pltpu.VMEM((KV_HEADS, TOK, GW), BF),
            pltpu.VMEM((GROUP * TOK, WINDOW * TOK), F32),
            pltpu.VMEM((GROUP * TOK, WINDOW * TOK), BF),
            pltpu.VMEM((GROUP * TOK, 1), F32),
        ],
        compiler_params=pltpu.CompilerParams(vmem_limit_bytes=VMEM),
        cost_estimate=HINT,
        name="attend",
    )(place, doc_col, expert_col, expert_row, queries, *blocks, *blocks, *blocks)


def gate_kernel(count, *refs):
    packs = refs[: 2 * count]
    w_refs = refs[2 * count : 2 * count + 2 * len(UNITS)]
    hidden, pre, rows = refs[2 * count + 2 * len(UNITS) :]
    step = pl.program_id(0)

    @pl.when(step == 0)
    def _():
        pre[...] = jnp.zeros_like(pre)

    for n in range(8):

        @pl.when(step == n)
        def _(n=n):
            h, o = n // FOLD, n % FOLD
            m = iota((EXPERTS * 2, PACK_ROWS), 0)
            c = iota((EXPERTS * 2, PACK_ROWS), 1)
            pick = (c == (m // 2) * MAIN + 2 * o + m % 2).astype(F32).astype(BF)
            for i in range(count):
                pack = packs[2 * i + h]
                lo = i * BLOCK_ROWS
                rows[lo : lo + PACK_ROWS, :] = pack[:, o * GW : (o + 1) * GW]
                rows[lo + PACK_ROWS : lo + BLOCK_ROWS, :] = dot(pick, pack[:, HALF:]).astype(BF)

    x = rows[...]
    for n, w in enumerate(w_refs):
        at = sum(UNITS[: n % len(UNITS)])
        units = slice(at, at + UNITS[n % len(UNITS)])
        pre[n // len(UNITS), units, :] += dot_t(w[...], x)

    @pl.when(step == 7)
    def _():
        for s in range(2):
            x = pre[s]
            hidden[s] = (x * (1.0 / (1.0 + jnp.exp(-x)))).T.astype(BF)


def gate(packs, weights):
    count = len(packs) // 2
    rows = count * BLOCK_ROWS
    return pl.pallas_call(
        lambda *refs: gate_kernel(count, *refs),
        grid=(8,),
        in_specs=[pl.BlockSpec((PACK_ROWS, HALF + GW), lambda i: (0, 0))] * (2 * count)
        + [pl.BlockSpec((units, GW), lambda i: (0, i)) for units in UNITS * 2],
        out_specs=pl.BlockSpec((2, rows, UNIT), lambda i: (0, 0, 0)),
        out_shape=jax.ShapeDtypeStruct((2, rows, UNIT), BF),
        scratch_shapes=[pltpu.VMEM((2, UNIT, rows), F32), pltpu.VMEM((rows, GW), BF)],
        compiler_params=pltpu.CompilerParams(vmem_limit_bytes=VMEM),
        cost_estimate=HINT,
        name="gate",
    )(*packs, *weights)


def down_kernel(count, part, hidden, kept, other, *refs):
    outs = refs[:count]
    extras = refs[count]
    step = pl.program_id(0)
    row = iota((PACK_ROWS, EXPERTS * 2), 0)
    m = iota((PACK_ROWS, EXPERTS * 2), 1)
    put = (row == (m // 2) * MAIN + 2 * step + m % 2).astype(F32).astype(BF)
    product = (dot(hidden[0], kept[...]) + dot(hidden[1], other[...])).astype(BF)
    lanes = pl.ds(pl.multiple_of(step * part, 128), part)
    for i in range(count):
        lo = i * BLOCK_ROWS
        outs[i][:, lanes] = product[lo : lo + PACK_ROWS]
        folded = dot(put, product[lo + PACK_ROWS : lo + BLOCK_ROWS])

        @pl.when(step == 0)
        def _(i=i, folded=folded):
            extras[i] = folded

        @pl.when(step > 0)
        def _(i=i, folded=folded):
            extras[i] += folded

        @pl.when(step == FOLD - 1)
        def _(i=i):
            outs[i][:, FOLD * part :] = extras[i].astype(BF)


def down(hidden, kept, other):
    rows = hidden.shape[1]
    columns = kept.shape[1]
    part = columns // FOLD
    count = rows // BLOCK_ROWS
    return pl.pallas_call(
        lambda *refs: down_kernel(count, part, *refs),
        grid=(FOLD,),
        in_specs=[pl.BlockSpec((2, rows, UNIT), lambda i: (0, 0, 0))]
        + [pl.BlockSpec((UNIT, part), lambda i: (0, i))] * 2,
        out_specs=[pl.BlockSpec((PACK_ROWS, columns + part), lambda i: (0, 0))] * count,
        out_shape=[jax.ShapeDtypeStruct((PACK_ROWS, columns + part), BF)] * count,
        scratch_shapes=[pltpu.VMEM((count, PACK_ROWS, part), F32)],
        compiler_params=pltpu.CompilerParams(vmem_limit_bytes=VMEM),
        cost_estimate=HINT,
        name="down",
    )(hidden, kept, other)


def combine_kernel(att_ref, *refs):
    backs = refs[: len(PIECES)]
    prob_ref, ecol_ref, erow_ref, out_ref = refs[len(PIECES) :]
    experts = ecol_ref[...]
    earlier = (erow_ref[...] == experts) & (iota((TOK, TOK), 1) < iota((TOK, TOK), 0))
    slot = experts * CAP + jnp.sum(earlier.astype(jnp.int32), axis=1, keepdims=True)
    col = iota((TOK, PACK_ROWS), 1)
    expert, r = col // MAIN, col % MAIN
    main_hot = (slot == expert * CAP + r).astype(F32).astype(BF)
    hit = slot == expert * CAP + MAIN + r % 2
    extra_hot = [(hit & (r // 2 == o)).astype(F32).astype(BF) for o in range(FOLD)]
    prob = prob_ref[...]
    at = 0
    for back, columns in zip(backs, PIECES):
        part = columns // FOLD
        for o in range(FOLD):
            y = dot(main_hot, back[:, o * part : (o + 1) * part])
            y += dot(extra_hot[o], back[:, columns:])
            cols = slice(at + o * part, at + (o + 1) * part)
            out_ref[:, cols] = (att_ref[:, cols].astype(F32) + prob * y).astype(BF)
        at += columns


def combine(attended, backs, prob, expert_col, expert_row):
    return pl.pallas_call(
        combine_kernel,
        out_shape=jax.ShapeDtypeStruct((TOK, D), BF),
        compiler_params=pltpu.CompilerParams(vmem_limit_bytes=VMEM),
        cost_estimate=HINT,
        name="combine",
    )(attended, *backs, prob, expert_col, expert_row)


def shift(x, by):
    return lax.ppermute(x, "z", [(i, (i + by) % 4) for i in range(4)])


def on_device(queries, keys_values, doc_ids, expert_ids, gate_probs, w_gate, w_down):
    z = lax.axis_index("z")
    place = lax.axis_index("xh") * 4 + z
    docs = doc_ids[0]
    own = jnp.concatenate(
        [keys_values[0], jnp.broadcast_to(docs.astype(BF)[None, :], (TOK, TOK))], axis=1
    )
    across = lax.ppermute(own, "xh", [(0, 1)])
    blocks = [own]
    for k in (1, 2, 3):
        blocks.append(shift(jnp.where(z + k >= 4, across, own), k))
    blocks.append(across)

    moves = []
    for xh in range(2):
        for xl in range(2):
            for core in range(2):
                moves.append((xh * 4 + xl * 2 + core, core * 4 + (1 - xl) * 2 + xh))

    def after(x, *earlier):
        return lax.optimization_barrier((x, *earlier))[0]

    def fetch(w):
        return lax.ppermute(w, ("xh", "xl", "core"), moves)

    def swap_cores(w):
        return lax.ppermute(w, "core", [(0, 1), (1, 0)])

    def cut(w, sizes, axis):
        at = 0
        for size in sizes:
            yield lax.slice_in_dim(w, at, at + size, axis=axis)
            at += size

    gate_pieces = list(cut(w_gate[0].T, UNITS, 0))
    down_pieces = list(cut(w_down[0], PIECES, 1))
    gate_1 = fetch(after(gate_pieces[0], across))

    expert_col = (expert_ids[0] + EXPERTS // 2) % EXPERTS
    expert_row = expert_col.reshape(1, TOK)
    heads, gate_1, gate_piece, blocks, down_pieces = lax.optimization_barrier(
        (queries[0], gate_1, gate_pieces[1], blocks, down_pieces)
    )
    gate_2 = fetch(gate_piece)
    other_1 = swap_cores(gate_1)
    attended, send = attend(
        place[None], docs.astype(F32).reshape(TOK, 1), expert_col, expert_row, heads, blocks
    )

    def exchange(x):
        shape = x.shape
        x = x.reshape(EXPERTS, -1, shape[1])
        return lax.all_to_all(x, PLANE, split_axis=0, concat_axis=0, tiled=True)

    def add(*xs):
        total = xs[0].astype(F32)
        for x in xs[1:]:
            total = total + x.astype(F32)
        return total.astype(BF)

    send, gate_2, other_1 = lax.optimization_barrier((send, gate_2, other_1))
    other_2 = swap_cores(gate_2)
    mine, other_2, gate_piece = lax.optimization_barrier((exchange(send), other_2, gate_pieces[2]))
    gate_3 = fetch(gate_piece)
    mine_a = mine[:, :MAIN].reshape(PACK_ROWS, HALF + GW)
    mine_b = mine[:, MAIN:].reshape(PACK_ROWS, HALF + GW)
    left_a, right_a = shift(mine_a, 1), shift(mine_a, -1)
    left_b, right_b = shift(mine_b, 1), shift(mine_b, -1)
    left_a, right_a, left_b, right_b, gate_3, *down_pieces = lax.optimization_barrier(
        (left_a, right_a, left_b, right_b, gate_3, *down_pieces)
    )
    far_a = shift(left_a, 1)
    far_b = shift(right_b, -1)
    other_3 = swap_cores(gate_3)
    kept = fetch(down_pieces[0])
    gate_weights = (gate_1, gate_2, gate_3, other_1, other_2, other_3)
    near = gate((left_a, left_b, right_a, right_b, mine_a, mine_b), gate_weights)
    far = gate((far_a, far_b), gate_weights)
    near, far, kept, *down_pieces = lax.optimization_barrier((near, far, kept, *down_pieces))

    backs = []
    for n in range(len(PIECES)):
        other = swap_cores(kept)
        if n + 1 < len(PIECES):
            following = fetch(after(down_pieces[n + 1], kept))
        (far_part,) = down(far, kept, other)
        left_part, right_part, own_part = down(near, kept, other)
        if n + 1 < len(PIECES):
            following = after(following, far_part, own_part)
        way = 1 if n == 0 else -1
        onward, direct = (right_part, left_part) if way == 1 else (left_part, right_part)
        chain = add(onward, shift(far_part, way))
        total = add(own_part, shift(chain, way), shift(direct, -way))
        backs.append(exchange(total).reshape(total.shape))
        kept = following
    out = combine(attended, backs, gate_probs[0], expert_col, expert_row)
    return out[None]


def solution(mesh):
    split = Mesh(mesh.devices.reshape(2, 4, 2, 4, 2), ("xh", "z", "xl", "y", "core"))
    ctx, exp = ("xh", "z"), ("xl", "y", "core")
    return jax.shard_map(
        on_device,
        mesh=split,
        in_specs=(
            P(exp, ctx, None),
            P(exp, ctx, None),
            P(exp, ctx),
            P(exp, ctx, None),
            P(exp, ctx, None),
            P(exp, None, ctx),
            P(exp, ctx, None),
        ),
        out_specs=P(exp, ctx, None),
        check_vma=False,
    )
```

```python
import math

import jax
import jax.numpy as jnp
from jax import lax
from jax.experimental import pallas as pl
from jax.experimental.pallas import tpu as pltpu
from jax.sharding import Mesh, PartitionSpec as P

D = 6144
HALF = D // 2
TOK = 128
KV_HEADS = 8
GROUP = 6
HW = 128
GW = GROUP * HW
WINDOW = 5
EXPERTS = 16
CAP = 10
MAIN = 8
FOLD = 4
UNIT = 672
PACK_ROWS = EXPERTS * MAIN
BLOCK_ROWS = EXPERTS * CAP
PIECES = (1536, 2560, 2048)
UNITS = (208, 128, 336)
VMEM = 50 * 1024 * 1024
PLANE = ("xl", "y", "xh")
BF = jnp.bfloat16
F32 = jnp.float32


def cost(microseconds):
    return pl.CostEstimate(flops=10**9 * microseconds, bytes_accessed=10**6, transcendentals=0)


def iota(shape, axis):
    return lax.broadcasted_iota(jnp.int32, shape, axis)


def dot(a, b):
    return jnp.dot(a, b, preferred_element_type=F32)


def dot_t(a, b):
    return lax.dot_general(a, b, (((1,), (1,)), ((), ())), preferred_element_type=F32)


def attend_kernel(place_ref, doc_ref, ecol_ref, erow_ref, q_ref, *refs):
    k_refs = refs[:WINDOW]
    v_refs = refs[WINDOW : 2 * WINDOW]
    d_refs = refs[2 * WINDOW : 3 * WINDOW]
    att_ref, send, bias, keys, values, held, scores, weights, totals = refs[3 * WINDOW :]
    head = pl.program_id(0)

    @pl.when(head == 0)
    def _():
        place = place_ref[0]
        mine = doc_ref[...]
        for n in range(WINDOW):
            same = mine == d_refs[n][...].astype(F32)
            if n == 0:
                ok = same & (iota((TOK, TOK), 1) <= iota((TOK, TOK), 0))
            else:
                ok = same & (iota((TOK, TOK), 0) * 0 + place >= n)
            bias[:, n * TOK : (n + 1) * TOK] = jnp.where(ok, 0.0, -1e30)

    for n in range(WINDOW):
        keys[n * TOK : (n + 1) * TOK, :] = k_refs[n][...]
        values[n * TOK : (n + 1) * TOK, :] = v_refs[n][...]
    stacked = jnp.concatenate([q_ref[:, i * HW : (i + 1) * HW] for i in range(GROUP)], axis=0)
    scores[...] = dot_t(stacked, keys[...])
    for i in range(GROUP):
        rows = slice(i * TOK, (i + 1) * TOK)
        s = scores[rows, :] * (math.log2(math.e) / math.sqrt(HW)) + bias[...]
        w = jnp.exp2(s - jnp.max(s, axis=1, keepdims=True))
        totals[rows, :] = jnp.sum(w, axis=1, keepdims=True)
        weights[rows, :] = w.astype(BF)
    blended = (dot(weights[...], values[...]) / totals[...]).astype(BF)
    for i in range(GROUP):
        o = blended[i * TOK : (i + 1) * TOK]
        att_ref[:, i * HW : (i + 1) * HW] = o
        held[head, :, i * HW : (i + 1) * HW] = o

    @pl.when(head == KV_HEADS - 1)
    def _():
        total = jnp.zeros((TOK, 1), F32)
        for g in range(KV_HEADS):
            total += jnp.sum(held[g].astype(F32), axis=1, keepdims=True)
        mean = total * (1.0 / D)
        square = jnp.zeros((TOK, 1), F32)
        for g in range(KV_HEADS):
            c = held[g].astype(F32) - mean
            square += jnp.sum(c * c, axis=1, keepdims=True)
        scale = lax.rsqrt(square * (1.0 / D) + 1e-05)
        for g in range(KV_HEADS):
            held[g] = ((held[g].astype(F32) - mean) * scale).astype(BF)
        experts = erow_ref[...]
        earlier = (ecol_ref[...] == experts) & (iota((TOK, TOK), 0) < iota((TOK, TOK), 1))
        slot = experts * CAP + jnp.sum(earlier.astype(jnp.int32), axis=0, keepdims=True)
        row = iota((2 * PACK_ROWS, TOK), 0)
        expert, half, r = row // (2 * MAIN), row // MAIN % 2, row % MAIN
        hit = slot == expert * CAP + r
        main_hot = jnp.concatenate(
            [(hit & (half == h)).astype(F32).astype(BF) for h in range(2)], axis=1
        )
        hit = slot == expert * CAP + MAIN + r % 2
        extra_hot = jnp.concatenate(
            [
                (hit & (half == n // FOLD) & (r // 2 == n % FOLD)).astype(F32).astype(BF)
                for n in range(KV_HEADS)
            ],
            axis=1,
        )
        for o in range(FOLD):
            pair = jnp.concatenate([held[o], held[FOLD + o]], axis=0)
            send[:, o * GW : (o + 1) * GW] = dot(main_hot, pair).astype(BF)
        every = jnp.concatenate([held[n] for n in range(KV_HEADS)], axis=0)
        send[:, HALF:] = dot(extra_hot, every).astype(BF)


def attend(place, doc_col, expert_col, expert_row, queries, blocks):
    def whole(shape):
        return pl.BlockSpec(shape, lambda g: (0, 0))

    in_specs = [
        pl.BlockSpec(memory_space=pltpu.SMEM),
        whole((TOK, 1)),
        whole((TOK, 1)),
        whole((1, TOK)),
        pl.BlockSpec((TOK, GW), lambda g: (0, g)),
    ]
    in_specs += [pl.BlockSpec((TOK, HW), lambda g: (0, g))] * WINDOW
    in_specs += [pl.BlockSpec((TOK, HW), lambda g: (0, KV_HEADS + g))] * WINDOW
    in_specs += [pl.BlockSpec((TOK, HW), lambda g: (0, 2 * KV_HEADS))] * WINDOW
    return pl.pallas_call(
        attend_kernel,
        grid=(KV_HEADS,),
        in_specs=in_specs,
        out_specs=[
            pl.BlockSpec((TOK, GW), lambda g: (0, g)),
            whole((2 * PACK_ROWS, HALF + GW)),
        ],
        out_shape=[
            jax.ShapeDtypeStruct((TOK, D), BF),
            jax.ShapeDtypeStruct((2 * PACK_ROWS, HALF + GW), BF),
        ],
        scratch_shapes=[
            pltpu.VMEM((TOK, WINDOW * TOK), F32),
            pltpu.VMEM((WINDOW * TOK, HW), BF),
            pltpu.VMEM((WINDOW * TOK, HW), BF),
            pltpu.VMEM((KV_HEADS, TOK, GW), BF),
            pltpu.VMEM((GROUP * TOK, WINDOW * TOK), F32),
            pltpu.VMEM((GROUP * TOK, WINDOW * TOK), BF),
            pltpu.VMEM((GROUP * TOK, 1), F32),
        ],
        compiler_params=pltpu.CompilerParams(vmem_limit_bytes=VMEM),
        cost_estimate=cost(16),
        name="attend",
    )(place, doc_col, expert_col, expert_row, queries, *blocks, *blocks, *blocks)


def gate_kernel(count, *refs):
    packs = refs[: 2 * count]
    w_refs = refs[2 * count : 2 * count + 2 * len(UNITS)]
    hidden, pre, rows = refs[2 * count + 2 * len(UNITS) :]
    step = pl.program_id(0)

    @pl.when(step == 0)
    def _():
        pre[...] = jnp.zeros_like(pre)

    for n in range(8):

        @pl.when(step == n)
        def _(n=n):
            h, o = n // FOLD, n % FOLD
            m = iota((EXPERTS * 2, PACK_ROWS), 0)
            c = iota((EXPERTS * 2, PACK_ROWS), 1)
            pick = (c == (m // 2) * MAIN + 2 * o + m % 2).astype(F32).astype(BF)
            for i in range(count):
                pack = packs[2 * i + h]
                lo = i * BLOCK_ROWS
                rows[lo : lo + PACK_ROWS, :] = pack[:, o * GW : (o + 1) * GW]
                rows[lo + PACK_ROWS : lo + BLOCK_ROWS, :] = dot(pick, pack[:, HALF:]).astype(BF)

    x = rows[...]
    for n, w in enumerate(w_refs):
        at = sum(UNITS[: n % len(UNITS)])
        units = slice(at, at + UNITS[n % len(UNITS)])
        pre[n // len(UNITS), units, :] += dot_t(w[...], x)

    @pl.when(step == 7)
    def _():
        for s in range(2):
            x = pre[s]
            hidden[s] = (x * (1.0 / (1.0 + jnp.exp(-x)))).T.astype(BF)


def gate(packs, weights):
    count = len(packs) // 2
    rows = count * BLOCK_ROWS
    pack_specs = [pl.BlockSpec((PACK_ROWS, HALF + GW), lambda i, at=at: (at, 0)) for _, at in packs]
    return pl.pallas_call(
        lambda *refs: gate_kernel(count, *refs),
        grid=(8,),
        in_specs=pack_specs
        + [pl.BlockSpec((units, GW), lambda i: (0, i)) for units in UNITS * 2],
        out_specs=pl.BlockSpec((2, rows, UNIT), lambda i: (0, 0, 0)),
        out_shape=jax.ShapeDtypeStruct((2, rows, UNIT), BF),
        scratch_shapes=[pltpu.VMEM((2, UNIT, rows), F32), pltpu.VMEM((rows, GW), BF)],
        compiler_params=pltpu.CompilerParams(vmem_limit_bytes=VMEM),
        cost_estimate=cost(8 + rows // 40),
        name="gate",
    )(*[pack for pack, _ in packs], *weights)


def down_kernel(count, part, fetches, hidden, *refs):
    w_refs = refs[: 2 * fetches]
    outs = refs[2 * fetches : 2 * fetches + count]
    extras = refs[2 * fetches + count]
    step = pl.program_id(0)
    row = iota((PACK_ROWS, EXPERTS * 2), 0)
    m = iota((PACK_ROWS, EXPERTS * 2), 1)
    put = (row == (m // 2) * MAIN + 2 * step + m % 2).astype(F32).astype(BF)
    if fetches == 1:
        kept, other = (w[...] for w in w_refs)
    else:
        late = step >= FOLD // 2
        kept = jnp.where(late, w_refs[1][...], w_refs[0][...])
        other = jnp.where(late, w_refs[3][...], w_refs[2][...])
    product = (dot(hidden[0], kept) + dot(hidden[1], other)).astype(BF)
    lanes = pl.ds(pl.multiple_of(step * part, 128), part)
    for i in range(count):
        lo = i * BLOCK_ROWS
        outs[i][:, lanes] = product[lo : lo + PACK_ROWS]
        folded = dot(put, product[lo + PACK_ROWS : lo + BLOCK_ROWS])

        @pl.when(step == 0)
        def _(i=i, folded=folded):
            extras[i] = folded

        @pl.when(step > 0)
        def _(i=i, folded=folded):
            extras[i] += folded

        @pl.when(step == FOLD - 1)
        def _(i=i):
            outs[i][:, FOLD * part :] = extras[i].astype(BF)


def down(hidden, kept, other, microseconds=0):
    kept, other = (kept,), (other,)
    rows = hidden.shape[1]
    fetches = len(kept)
    columns = sum(w.shape[1] for w in kept)
    part = columns // FOLD
    count = rows // BLOCK_ROWS
    if fetches == 1:
        w_specs = [pl.BlockSpec((UNIT, part), lambda i: (0, i))]
    else:
        w_specs = [
            pl.BlockSpec((UNIT, part), lambda i: (0, jnp.minimum(i, 1))),
            pl.BlockSpec((UNIT, part), lambda i: (0, jnp.maximum(i - 2, 0))),
        ]
    return pl.pallas_call(
        lambda *refs: down_kernel(count, part, fetches, *refs),
        grid=(FOLD,),
        in_specs=[pl.BlockSpec((2, rows, UNIT), lambda i: (0, 0, 0))] + w_specs * 2,
        out_specs=[pl.BlockSpec((PACK_ROWS, columns + part), lambda i: (0, 0))] * count,
        out_shape=[jax.ShapeDtypeStruct((PACK_ROWS, columns + part), BF)] * count,
        scratch_shapes=[pltpu.VMEM((count, PACK_ROWS, part), F32)],
        compiler_params=pltpu.CompilerParams(vmem_limit_bytes=VMEM),
        cost_estimate=cost(microseconds),
        name="down",
    )(hidden, *kept, *other)


def combine_kernel(att_ref, *refs):
    first, second, prob_ref, ecol_ref, erow_ref, out_ref = refs
    split = PIECES[1] + PIECES[1] // FOLD
    backs = (first, second.at[:, :split], second.at[:, split:])
    experts = ecol_ref[...]
    earlier = (erow_ref[...] == experts) & (iota((TOK, TOK), 1) < iota((TOK, TOK), 0))
    slot = experts * CAP + jnp.sum(earlier.astype(jnp.int32), axis=1, keepdims=True)
    col = iota((TOK, PACK_ROWS), 1)
    expert, r = col // MAIN, col % MAIN
    main_hot = (slot == expert * CAP + r).astype(F32).astype(BF)
    hit = slot == expert * CAP + MAIN + r % 2
    extra_hot = [(hit & (r // 2 == o)).astype(F32).astype(BF) for o in range(FOLD)]
    prob = prob_ref[...]
    at = 0
    for back, columns in zip(backs, PIECES):
        part = columns // FOLD
        for o in range(FOLD):
            y = dot(main_hot, back[:, o * part : (o + 1) * part])
            y += dot(extra_hot[o], back[:, columns:])
            cols = slice(at + o * part, at + (o + 1) * part)
            out_ref[:, cols] = (att_ref[:, cols].astype(F32) + prob * y).astype(BF)
        at += columns


def combine(attended, backs, prob, expert_col, expert_row):
    return pl.pallas_call(
        combine_kernel,
        out_shape=jax.ShapeDtypeStruct((TOK, D), BF),
        compiler_params=pltpu.CompilerParams(vmem_limit_bytes=VMEM),
        cost_estimate=cost(3),
        name="combine",
    )(attended, *backs, prob, expert_col, expert_row)


def shift(x, by):
    return lax.ppermute(x, "z", [(i, (i + by) % 4) for i in range(4)])


def on_device(queries, keys_values, doc_ids, expert_ids, gate_probs, w_gate, w_down):
    z = lax.axis_index("z")
    place = lax.axis_index("xh") * 4 + z
    docs = doc_ids[0]
    own = jnp.concatenate(
        [keys_values[0], jnp.broadcast_to(docs.astype(BF)[None, :], (TOK, TOK))], axis=1
    )
    across = lax.ppermute(own, "xh", [(0, 1)])
    blocks = [own]
    for k in (1, 2, 3):
        blocks.append(shift(jnp.where(z + k >= 4, across, own), k))
    blocks.append(across)

    moves = []
    for xh in range(2):
        for xl in range(2):
            for core in range(2):
                moves.append((xh * 4 + xl * 2 + core, core * 4 + (1 - xl) * 2 + xh))

    barrier = lax.optimization_barrier

    def after(x, *earlier):
        return lax.optimization_barrier((x, *earlier))[0]

    def fetch(w):
        return lax.ppermute(w, ("xh", "xl", "core"), moves)

    def swap_cores(w):
        return lax.ppermute(w, "core", [(0, 1), (1, 0)])

    def cut(w, sizes, axis):
        at = 0
        for size in sizes:
            yield lax.slice_in_dim(w, at, at + size, axis=axis)
            at += size

    gate_pieces = list(cut(w_gate[0].T, UNITS, 0))
    down_pieces = list(cut(w_down[0], PIECES, 1))
    gate_1 = fetch(after(gate_pieces[0], across))

    expert_col = (expert_ids[0] + EXPERTS // 2) % EXPERTS
    expert_row = expert_col.reshape(1, TOK)
    heads, gate_1, gate_piece, blocks, down_pieces = lax.optimization_barrier(
        (queries[0], gate_1, gate_pieces[1], blocks, down_pieces)
    )
    gate_2 = fetch(gate_piece)
    other_1 = swap_cores(gate_1)
    attended, send = attend(
        place[None], docs.astype(F32).reshape(TOK, 1), expert_col, expert_row, heads, blocks
    )

    def exchange(x):
        shape = x.shape
        x = x.reshape(EXPERTS, -1, shape[1])
        return lax.all_to_all(x, PLANE, split_axis=0, concat_axis=0, tiled=True)

    def add(*xs):
        total = xs[0].astype(F32)
        for x in xs[1:]:
            total = total + x.astype(F32)
        return total.astype(BF)

    send, gate_2, other_1 = lax.optimization_barrier((send, gate_2, other_1))
    other_2 = swap_cores(gate_2)
    back, other_2, gate_piece = lax.optimization_barrier((exchange(send), other_2, gate_pieces[2]))
    mine = back.reshape(EXPERTS, 2, MAIN, HALF + GW).transpose(1, 0, 2, 3)
    mine = mine.reshape(2 * PACK_ROWS, HALF + GW)
    gate_3 = fetch(gate_piece)
    left, right, gate_3, down_pieces = lax.optimization_barrier(
        (shift(mine, 1), shift(mine, -1), gate_3, down_pieces)
    )
    far_a = shift(left[:PACK_ROWS], 1)
    far_b = shift(right[PACK_ROWS:], -1)
    other_3 = swap_cores(gate_3)
    kept_a = fetch(down_pieces[0])
    gate_weights = (gate_1, gate_2, gate_3, other_1, other_2, other_3)
    near = gate([(x, at) for x in (left, right, mine) for at in range(2)], gate_weights)
    near, far_a, far_b, kept_a, down_pieces = barrier((near, far_a, far_b, kept_a, down_pieces))
    far = gate([(far_a, 0), (far_b, 0)], gate_weights)
    kept_b = fetch(down_pieces[1])
    other_a = swap_cores(kept_a)
    far, other_a, down_pieces = barrier((far, other_a, down_pieces))

    (far_part,) = down(far, kept_a, other_a, 4)
    left_part, right_part, own_a = down(after(near, far_part), kept_a, other_a, 8)
    passed, direct_a, right_part, kept_b = barrier(
        (shift(far_part, 1), shift(left_part, -1), right_part, kept_b)
    )
    kept_c = fetch(after(down_pieces[2], kept_b))
    other_b = swap_cores(kept_b)
    chain_a = add(right_part, passed)
    (far_part,) = down(far, kept_b, other_b, 4)
    left_part, right_part, own_b = down(after(near, far_part), kept_b, other_b, 8)
    summed_a, passed, left_part, right_part, kept_c = barrier(
        (shift(chain_a, 1), shift(far_part, -1), left_part, right_part, kept_c)
    )
    other_c = swap_cores(kept_c)
    back_a = exchange(add(own_a, summed_a, direct_a))
    chain_b = add(left_part, passed)
    (far_c,) = down(far, kept_c, other_c, 3)
    left_c, right_c, own_c = down(after(near, far_c), kept_c, other_c, 6)
    summed_b, direct_b, far_c, left_c, right_c, back_a = barrier(
        (
            shift(chain_b, -1),
            shift(right_part, 1),
            shift(far_c, 2),
            shift(left_c, -1),
            shift(right_c, 1),
            back_a,
        )
    )
    total_b = add(own_b, summed_b, direct_b)
    total_c = add(own_c, far_c, left_c, right_c)
    backs = [back_a, exchange(jnp.concatenate([total_b, total_c], axis=1))]
    backs = [back.reshape(PACK_ROWS, -1) for back in backs]
    out = combine(attended, backs, gate_probs[0], expert_col, expert_row)
    return out[None]


def solution(mesh):
    split = Mesh(mesh.devices.reshape(2, 4, 2, 4, 2), ("xh", "z", "xl", "y", "core"))
    ctx, exp = ("xh", "z"), ("xl", "y", "core")
    return jax.shard_map(
        on_device,
        mesh=split,
        in_specs=(
            P(exp, ctx, None),
            P(exp, ctx, None),
            P(exp, ctx),
            P(exp, ctx, None),
            P(exp, ctx, None),
            P(exp, None, ctx),
            P(exp, ctx, None),
        ),
        out_specs=P(exp, ctx, None),
        check_vma=False,
    )
```

```python
import math

import jax
import jax.numpy as jnp
from jax import lax
from jax.experimental import pallas as pl
from jax.experimental.pallas import tpu as pltpu
from jax.sharding import Mesh, PartitionSpec as P

D = 6144
HALF = D // 2
TOK = 128
KV_HEADS = 8
GROUP = 6
HW = 128
GW = GROUP * HW
WINDOW = 5
EXPERTS = 16
CAP = 10
MAIN = 8
FOLD = 4
UNIT = 672
PACK_ROWS = EXPERTS * MAIN
BLOCK_ROWS = EXPERTS * CAP
PIECES = (1536, 2560, 2048)
UNITS = (208, 128, 336)
VMEM = 50 * 1024 * 1024
PLANE = ("xl", "y", "xh")
BF = jnp.bfloat16
F32 = jnp.float32


def cost(microseconds):
    return pl.CostEstimate(flops=10**9 * microseconds, bytes_accessed=10**6, transcendentals=0)


def iota(shape, axis):
    return lax.broadcasted_iota(jnp.int32, shape, axis)


def dot(a, b):
    return jnp.dot(a, b, preferred_element_type=F32)


def dot_t(a, b):
    return lax.dot_general(a, b, (((1,), (1,)), ((), ())), preferred_element_type=F32)


def attend_kernel(place_ref, doc_ref, ecol_ref, erow_ref, q_ref, *refs):
    k_refs = refs[:WINDOW]
    v_refs = refs[WINDOW : 2 * WINDOW]
    d_refs = refs[2 * WINDOW : 3 * WINDOW]
    att_ref, send, bias, keys, values, held, scores, weights, totals = refs[3 * WINDOW :]
    head = pl.program_id(0)

    @pl.when(head == 0)
    def _():
        place = place_ref[0]
        mine = doc_ref[...]
        for n in range(WINDOW):
            same = mine == d_refs[n][...].astype(F32)
            if n == 0:
                ok = same & (iota((TOK, TOK), 1) <= iota((TOK, TOK), 0))
            else:
                ok = same & (iota((TOK, TOK), 0) * 0 + place >= n)
            bias[:, n * TOK : (n + 1) * TOK] = jnp.where(ok, 0.0, -1e30)

    for n in range(WINDOW):
        keys[n * TOK : (n + 1) * TOK, :] = k_refs[n][...]
        values[n * TOK : (n + 1) * TOK, :] = v_refs[n][...]
    stacked = jnp.concatenate([q_ref[:, i * HW : (i + 1) * HW] for i in range(GROUP)], axis=0)
    scores[...] = dot_t(stacked, keys[...])
    for i in range(GROUP):
        rows = slice(i * TOK, (i + 1) * TOK)
        s = scores[rows, :] * (math.log2(math.e) / math.sqrt(HW)) + bias[...]
        w = jnp.exp2(s - jnp.max(s, axis=1, keepdims=True))
        totals[rows, :] = jnp.sum(w, axis=1, keepdims=True)
        weights[rows, :] = w.astype(BF)
    blended = (dot(weights[...], values[...]) / totals[...]).astype(BF)
    for i in range(GROUP):
        o = blended[i * TOK : (i + 1) * TOK]
        att_ref[:, i * HW : (i + 1) * HW] = o
        held[head, :, i * HW : (i + 1) * HW] = o

    @pl.when(head == KV_HEADS - 1)
    def _():
        total = jnp.zeros((TOK, 1), F32)
        for g in range(KV_HEADS):
            total += jnp.sum(held[g].astype(F32), axis=1, keepdims=True)
        mean = total * (1.0 / D)
        square = jnp.zeros((TOK, 1), F32)
        for g in range(KV_HEADS):
            c = held[g].astype(F32) - mean
            square += jnp.sum(c * c, axis=1, keepdims=True)
        scale = lax.rsqrt(square * (1.0 / D) + 1e-05)
        for g in range(KV_HEADS):
            held[g] = ((held[g].astype(F32) - mean) * scale).astype(BF)
        experts = erow_ref[...]
        earlier = (ecol_ref[...] == experts) & (iota((TOK, TOK), 0) < iota((TOK, TOK), 1))
        slot = experts * CAP + jnp.sum(earlier.astype(jnp.int32), axis=0, keepdims=True)
        row = iota((2 * PACK_ROWS, TOK), 0)
        expert, half, r = row // (2 * MAIN), row // MAIN % 2, row % MAIN
        hit = slot == expert * CAP + r
        main_hot = jnp.concatenate(
            [(hit & (half == h)).astype(F32).astype(BF) for h in range(2)], axis=1
        )
        hit = slot == expert * CAP + MAIN + r % 2
        extra_hot = jnp.concatenate(
            [
                (hit & (half == n // FOLD) & (r // 2 == n % FOLD)).astype(F32).astype(BF)
                for n in range(KV_HEADS)
            ],
            axis=1,
        )
        for o in range(FOLD):
            pair = jnp.concatenate([held[o], held[FOLD + o]], axis=0)
            send[:, o * GW : (o + 1) * GW] = dot(main_hot, pair).astype(BF)
        every = jnp.concatenate([held[n] for n in range(KV_HEADS)], axis=0)
        send[:, HALF:] = dot(extra_hot, every).astype(BF)


def attend(place, doc_col, expert_col, expert_row, queries, blocks):
    def whole(shape):
        return pl.BlockSpec(shape, lambda g: (0, 0))

    in_specs = [
        pl.BlockSpec(memory_space=pltpu.SMEM),
        whole((TOK, 1)),
        whole((TOK, 1)),
        whole((1, TOK)),
        pl.BlockSpec((TOK, GW), lambda g: (0, g)),
    ]
    in_specs += [pl.BlockSpec((TOK, HW), lambda g: (0, g))] * WINDOW
    in_specs += [pl.BlockSpec((TOK, HW), lambda g: (0, KV_HEADS + g))] * WINDOW
    in_specs += [pl.BlockSpec((TOK, HW), lambda g: (0, 2 * KV_HEADS))] * WINDOW
    return pl.pallas_call(
        attend_kernel,
        grid=(KV_HEADS,),
        in_specs=in_specs,
        out_specs=[
            pl.BlockSpec((TOK, GW), lambda g: (0, g)),
            whole((2 * PACK_ROWS, HALF + GW)),
        ],
        out_shape=[
            jax.ShapeDtypeStruct((TOK, D), BF),
            jax.ShapeDtypeStruct((2 * PACK_ROWS, HALF + GW), BF),
        ],
        scratch_shapes=[
            pltpu.VMEM((TOK, WINDOW * TOK), F32),
            pltpu.VMEM((WINDOW * TOK, HW), BF),
            pltpu.VMEM((WINDOW * TOK, HW), BF),
            pltpu.VMEM((KV_HEADS, TOK, GW), BF),
            pltpu.VMEM((GROUP * TOK, WINDOW * TOK), F32),
            pltpu.VMEM((GROUP * TOK, WINDOW * TOK), BF),
            pltpu.VMEM((GROUP * TOK, 1), F32),
        ],
        compiler_params=pltpu.CompilerParams(vmem_limit_bytes=VMEM),
        cost_estimate=cost(16),
        name="attend",
    )(place, doc_col, expert_col, expert_row, queries, *blocks, *blocks, *blocks)


def gate_kernel(count, *refs):
    packs = refs[: 2 * count]
    w_refs = refs[2 * count : 2 * count + 2 * len(UNITS)]
    hidden, pre, rows = refs[2 * count + 2 * len(UNITS) :]
    step = pl.program_id(0)

    @pl.when(step == 0)
    def _():
        pre[...] = jnp.zeros_like(pre)

    for n in range(4):

        @pl.when(step == n)
        def _(n=n):
            h = n // 2
            m = iota((EXPERTS * 2, PACK_ROWS), 0)
            c = iota((EXPERTS * 2, PACK_ROWS), 1)
            for p in range(2):
                o = 2 * (n % 2) + p
                cols = slice(p * GW, (p + 1) * GW)
                pick = (c == (m // 2) * MAIN + 2 * o + m % 2).astype(F32).astype(BF)
                for i in range(count):
                    pack = packs[2 * i + h]
                    lo = i * BLOCK_ROWS
                    rows[lo : lo + PACK_ROWS, cols] = pack[:, o * GW : (o + 1) * GW]
                    rows[lo + PACK_ROWS : lo + BLOCK_ROWS, cols] = dot(pick, pack[:, HALF:]).astype(BF)

    x = rows[...]
    for n, w in enumerate(w_refs):
        at = sum(UNITS[: n % len(UNITS)])
        units = slice(at, at + UNITS[n % len(UNITS)])
        pre[n // len(UNITS), units, :] += dot_t(w[...], x)

    @pl.when(step == 3)
    def _():
        for s in range(2):
            x = pre[s]
            hidden[s] = (x * (1.0 / (1.0 + jnp.exp(-x)))).T.astype(BF)


def gate(packs, weights):
    count = len(packs) // 2
    rows = count * BLOCK_ROWS
    pack_specs = [pl.BlockSpec((PACK_ROWS, HALF + GW), lambda i, at=at: (at, 0)) for _, at in packs]
    return pl.pallas_call(
        lambda *refs: gate_kernel(count, *refs),
        grid=(4,),
        in_specs=pack_specs
        + [pl.BlockSpec((units, 2 * GW), lambda i: (0, i)) for units in UNITS * 2],
        out_specs=pl.BlockSpec((2, rows, UNIT), lambda i: (0, 0, 0)),
        out_shape=jax.ShapeDtypeStruct((2, rows, UNIT), BF),
        scratch_shapes=[pltpu.VMEM((2, UNIT, rows), F32), pltpu.VMEM((rows, 2 * GW), BF)],
        compiler_params=pltpu.CompilerParams(vmem_limit_bytes=VMEM),
        cost_estimate=cost(8 + rows // 40),
        name="gate",
    )(*[pack for pack, _ in packs], *weights)


def down_kernel(count, part, fetches, hidden, *refs):
    w_refs = refs[: 2 * fetches]
    outs = refs[2 * fetches : 2 * fetches + count]
    extras = refs[2 * fetches + count]
    step = pl.program_id(0)
    row = iota((PACK_ROWS, EXPERTS * 2), 0)
    m = iota((PACK_ROWS, EXPERTS * 2), 1)
    put = (row == (m // 2) * MAIN + 2 * step + m % 2).astype(F32).astype(BF)
    if fetches == 1:
        kept, other = (w[...] for w in w_refs)
    else:
        late = step >= FOLD // 2
        kept = jnp.where(late, w_refs[1][...], w_refs[0][...])
        other = jnp.where(late, w_refs[3][...], w_refs[2][...])
    product = (dot(hidden[0], kept) + dot(hidden[1], other)).astype(BF)
    lanes = pl.ds(pl.multiple_of(step * part, 128), part)
    for i in range(count):
        lo = i * BLOCK_ROWS
        outs[i][:, lanes] = product[lo : lo + PACK_ROWS]
        folded = dot(put, product[lo + PACK_ROWS : lo + BLOCK_ROWS])

        @pl.when(step == 0)
        def _(i=i, folded=folded):
            extras[i] = folded

        @pl.when(step > 0)
        def _(i=i, folded=folded):
            extras[i] += folded

        @pl.when(step == FOLD - 1)
        def _(i=i):
            outs[i][:, FOLD * part :] = extras[i].astype(BF)


def down(hidden, kept, other, microseconds=0):
    kept, other = (kept,), (other,)
    rows = hidden.shape[1]
    fetches = len(kept)
    columns = sum(w.shape[1] for w in kept)
    part = columns // FOLD
    count = rows // BLOCK_ROWS
    if fetches == 1:
        w_specs = [pl.BlockSpec((UNIT, part), lambda i: (0, i))]
    else:
        w_specs = [
            pl.BlockSpec((UNIT, part), lambda i: (0, jnp.minimum(i, 1))),
            pl.BlockSpec((UNIT, part), lambda i: (0, jnp.maximum(i - 2, 0))),
        ]
    return pl.pallas_call(
        lambda *refs: down_kernel(count, part, fetches, *refs),
        grid=(FOLD,),
        in_specs=[pl.BlockSpec((2, rows, UNIT), lambda i: (0, 0, 0))] + w_specs * 2,
        out_specs=[pl.BlockSpec((PACK_ROWS, columns + part), lambda i: (0, 0))] * count,
        out_shape=[jax.ShapeDtypeStruct((PACK_ROWS, columns + part), BF)] * count,
        scratch_shapes=[pltpu.VMEM((count, PACK_ROWS, part), F32)],
        compiler_params=pltpu.CompilerParams(vmem_limit_bytes=VMEM),
        cost_estimate=cost(microseconds),
        name="down",
    )(hidden, *kept, *other)


def combine_kernel(att_ref, *refs):
    first, second, prob_ref, ecol_ref, erow_ref, out_ref = refs
    split = PIECES[1] + PIECES[1] // FOLD
    backs = (first, second.at[:, :split], second.at[:, split:])
    experts = ecol_ref[...]
    earlier = (erow_ref[...] == experts) & (iota((TOK, TOK), 1) < iota((TOK, TOK), 0))
    slot = experts * CAP + jnp.sum(earlier.astype(jnp.int32), axis=1, keepdims=True)
    col = iota((TOK, PACK_ROWS), 1)
    expert, r = col // MAIN, col % MAIN
    main_hot = (slot == expert * CAP + r).astype(F32).astype(BF)
    hit = slot == expert * CAP + MAIN + r % 2
    extra_hot = [(hit & (r // 2 == o)).astype(F32).astype(BF) for o in range(FOLD)]
    prob = prob_ref[...]
    at = 0
    for back, columns in zip(backs, PIECES):
        part = columns // FOLD
        for o in range(FOLD):
            y = dot(main_hot, back[:, o * part : (o + 1) * part])
            y += dot(extra_hot[o], back[:, columns:])
            cols = slice(at + o * part, at + (o + 1) * part)
            out_ref[:, cols] = (att_ref[:, cols].astype(F32) + prob * y).astype(BF)
        at += columns


def combine(attended, backs, prob, expert_col, expert_row):
    return pl.pallas_call(
        combine_kernel,
        out_shape=jax.ShapeDtypeStruct((TOK, D), BF),
        compiler_params=pltpu.CompilerParams(vmem_limit_bytes=VMEM),
        cost_estimate=cost(3),
        name="combine",
    )(attended, *backs, prob, expert_col, expert_row)


def shift(x, by):
    return lax.ppermute(x, "z", [(i, (i + by) % 4) for i in range(4)])


def on_device(queries, keys_values, doc_ids, expert_ids, gate_probs, w_gate, w_down):
    z = lax.axis_index("z")
    place = lax.axis_index("xh") * 4 + z
    docs = doc_ids[0]
    own = jnp.concatenate(
        [keys_values[0], jnp.broadcast_to(docs.astype(BF)[None, :], (TOK, TOK))], axis=1
    )
    across = lax.ppermute(own, "xh", [(0, 1)])
    blocks = [own]
    for k in (1, 2, 3):
        blocks.append(shift(jnp.where(z + k >= 4, across, own), k))
    blocks.append(across)

    moves = []
    for xh in range(2):
        for xl in range(2):
            for core in range(2):
                moves.append((xh * 4 + xl * 2 + core, core * 4 + (1 - xl) * 2 + xh))

    barrier = lax.optimization_barrier

    def after(x, *earlier):
        return lax.optimization_barrier((x, *earlier))[0]

    def fetch(w):
        return lax.ppermute(w, ("xh", "xl", "core"), moves)

    def swap_cores(w):
        return lax.ppermute(w, "core", [(0, 1), (1, 0)])

    def cut(w, sizes, axis):
        at = 0
        for size in sizes:
            yield lax.slice_in_dim(w, at, at + size, axis=axis)
            at += size

    gate_pieces = list(cut(w_gate[0].T, UNITS, 0))
    down_pieces = list(cut(w_down[0], PIECES, 1))
    gate_1 = fetch(after(gate_pieces[0], across))

    expert_col = (expert_ids[0] + EXPERTS // 2) % EXPERTS
    expert_row = expert_col.reshape(1, TOK)
    heads, gate_1, gate_piece, blocks, down_pieces = lax.optimization_barrier(
        (queries[0], gate_1, gate_pieces[1], blocks, down_pieces)
    )
    gate_2 = fetch(gate_piece)
    other_1 = swap_cores(gate_1)
    attended, send = attend(
        place[None], docs.astype(F32).reshape(TOK, 1), expert_col, expert_row, heads, blocks
    )

    def exchange(x):
        shape = x.shape
        x = x.reshape(EXPERTS, -1, shape[1])
        return lax.all_to_all(x, PLANE, split_axis=0, concat_axis=0, tiled=True)

    def add(*xs):
        total = xs[0].astype(F32)
        for x in xs[1:]:
            total = total + x.astype(F32)
        return total.astype(BF)

    send, gate_2, other_1 = lax.optimization_barrier((send, gate_2, other_1))
    other_2 = swap_cores(gate_2)
    back, other_2, gate_piece = lax.optimization_barrier((exchange(send), other_2, gate_pieces[2]))
    mine = back.reshape(EXPERTS, 2, MAIN, HALF + GW).transpose(1, 0, 2, 3)
    mine = mine.reshape(2 * PACK_ROWS, HALF + GW)
    gate_3 = fetch(gate_piece)
    left, right, gate_3, down_pieces = lax.optimization_barrier(
        (shift(mine, 1), shift(mine, -1), gate_3, down_pieces)
    )
    far_a = shift(left[:PACK_ROWS], 1)
    far_b = shift(right[PACK_ROWS:], -1)
    other_3 = swap_cores(gate_3)
    kept_a = fetch(down_pieces[0])
    gate_weights = (gate_1, gate_2, gate_3, other_1, other_2, other_3)
    near = gate([(x, at) for x in (left, right, mine) for at in range(2)], gate_weights)
    near, far_a, far_b, kept_a, down_pieces = barrier((near, far_a, far_b, kept_a, down_pieces))
    far = gate([(far_a, 0), (far_b, 0)], gate_weights)
    kept_b = fetch(down_pieces[1])
    other_a = swap_cores(kept_a)
    far, other_a, down_pieces = barrier((far, other_a, down_pieces))

    (far_part,) = down(far, kept_a, other_a, 4)
    left_part, right_part, own_a = down(after(near, far_part), kept_a, other_a, 8)
    passed, direct_a, right_part, kept_b = barrier(
        (shift(far_part, 1), shift(left_part, -1), right_part, kept_b)
    )
    kept_c = fetch(after(down_pieces[2], kept_b))
    other_b = swap_cores(kept_b)
    chain_a = add(right_part, passed)
    (far_part,) = down(far, kept_b, other_b, 4)
    left_part, right_part, own_b = down(after(near, far_part), kept_b, other_b, 8)
    summed_a, passed, left_part, right_part, kept_c = barrier(
        (shift(chain_a, 1), shift(far_part, -1), left_part, right_part, kept_c)
    )
    other_c = swap_cores(kept_c)
    back_a = exchange(add(own_a, summed_a, direct_a))
    chain_b = add(left_part, passed)
    (far_c,) = down(far, kept_c, other_c, 3)
    left_c, right_c, own_c = down(after(near, far_c), kept_c, other_c, 6)
    summed_b, direct_b, far_c, left_c, right_c, back_a = barrier(
        (
            shift(chain_b, -1),
            shift(right_part, 1),
            shift(far_c, 2),
            shift(left_c, -1),
            shift(right_c, 1),
            back_a,
        )
    )
    total_b = add(own_b, summed_b, direct_b)
    total_c = add(own_c, far_c, left_c, right_c)
    backs = [back_a, exchange(jnp.concatenate([total_b, total_c], axis=1))]
    backs = [back.reshape(PACK_ROWS, -1) for back in backs]
    out = combine(attended, backs, gate_probs[0], expert_col, expert_row)
    return out[None]


def solution(mesh):
    split = Mesh(mesh.devices.reshape(2, 4, 2, 4, 2), ("xh", "z", "xl", "y", "core"))
    ctx, exp = ("xh", "z"), ("xl", "y", "core")
    return jax.shard_map(
        on_device,
        mesh=split,
        in_specs=(
            P(exp, ctx, None),
            P(exp, ctx, None),
            P(exp, ctx),
            P(exp, ctx, None),
            P(exp, ctx, None),
            P(exp, None, ctx),
            P(exp, ctx, None),
        ),
        out_specs=P(exp, ctx, None),
        check_vma=False,
    )
```
